32 devices in a mesh: fsdp: 4 (over x, core), tp: 8 (over z, y).
Axes of the slice: x: 2, y: 2, z: 4, core: 2. Of those that a mesh axis runs over, the one named last changes fastest.
Arguments:
- tokens: bfloat16 [1024, 2560], P(('fsdp', 'tp')), may hold values from -6 to 6
- cotangent: bfloat16 [1024, 14336], P('fsdp', 'tp'), may hold values from -48 to 48
- up_branch: bfloat16 [1024, 14336], P('fsdp', 'tp'), may hold values from -6 to 6
- gate_weight: bfloat16 [2560, 14336], P('fsdp', 'tp'), may hold values from -0.125 to 0.125
- probe: bfloat16 [2560, 14336], P('fsdp', 'tp'), may hold values from -5 to 5
- hess_ema: float32 [2560, 14336], P('fsdp', 'tp'), may hold values from -6 to 6
Outputs:
- hess_diag: float32 [2560, 14336], P('fsdp', 'tp')
- ema_next: float32 [2560, 14336], P('fsdp', 'tp')
The draws below stay inside these ranges and needn't reach their ends.
All inputs are finite; a program needn't handle non-finite values.
Results may differ from the reference program's by a relative error of at most 0.015.
Values may be sent and summed in bfloat16 or wider, within the bound.
A program may use at most 128 MiB of HBM per device.

```python
import jax
import jax.numpy as jnp
from jax import lax

D = 2560
FF = 14336
TOKENS = 1024
N_FSDP = 4


def spiked(entries, stream_key, source, target, blocks, factor):
    owner, partner = [(jnp.arange(entries.shape[axis_at]) // (entries.shape[axis_at] // blocks)).reshape([-1 if axis == axis_at else 1 for axis in range(entries.ndim)]) for axis_at in (source, target)]
    chosen = jax.random.permutation(stream_key, blocks)[partner]
    strong = (owner == chosen) | (owner == (partner + blocks // 2) % blocks)
    return jnp.where(strong, factor * entries, entries)


def shard_levels(key, extent, split, low, top_value):
    def one(axis_at, shards_of):
        heights = jax.random.uniform(jax.random.fold_in(jax.random.fold_in(key, 6), axis_at), (shards_of,), jnp.float32, low / len(split), top_value / len(split))
        return jnp.repeat(jnp.exp(heights), extent[axis_at] // shards_of).reshape((-1,) + (1,) * (len(extent) - axis_at - 1))

    level = one(*split[0])
    for cut in split[1:]:
        level = level * one(*cut)
    return level


def bell_draw(stream_key, shape, width, bound, cuts=(), held_as=jnp.bfloat16):
    values = jax.random.normal(stream_key, shape, jnp.float32) * width
    if len(cuts) > 0:
        values = shard_levels(stream_key, shape, cuts, -0.22, 0.18) * values
    return jnp.clip(values, min=-bound, max=bound).astype(held_as)


def heavy_noise(rng, dims, scale, limit, cuts, heavy, kind=jnp.bfloat16):
    result = scale * jax.random.normal(rng, dims, jnp.float32)
    if cuts:
        result = result * shard_levels(rng, dims, cuts, -0.22, 0.18)
    return jnp.clip(spiked(result, jax.random.fold_in(rng, 3), *heavy), -limit, limit).astype(kind)


def setup_inputs(seed: int = 0) -> dict:
    key_list = jax.random.split(jax.random.key(seed), 7)
    return {
        "tokens": heavy_noise(key_list[0], (TOKENS, D), 1.0, 6.0, ((0, 32),), (0, 1, 32, 2.75)),
        "cotangent": bell_draw(key_list[1], (TOKENS, FF), 8.0, 48.0, ((0, 4), (1, 8))),
        "up_branch": bell_draw(key_list[2], (TOKENS, FF), 1.0, 6.0, ((0, 4), (1, 8))),
        "gate_weight": bell_draw(key_list[3], (D, FF), D ** -0.5, 0.125, ((0, 4), (1, 8))),
        "probe": bell_draw(key_list[4], (D, FF), 1.0, 5.0, ((0, 4), (1, 8))),
        "hess_ema": bell_draw(key_list[5], (D, FF), 1.0, 6.0, ((0, 4), (1, 8)), jnp.float32),
    }


def reference(tokens, cotangent, up_branch, gate_weight, probe, hess_ema):
    block = FF // 8
    count = FF // block
    group = TOKENS // N_FSDP

    def one_block(index):
        start = (index * block).astype(jnp.int32)
        weight_cols = lax.dynamic_slice_in_dim(gate_weight, start, block, 1)
        probe_cols = lax.dynamic_slice_in_dim(probe, start, block, 1)
        cot_cols = lax.dynamic_slice_in_dim(cotangent, start, block, 1)
        up_cols = lax.dynamic_slice_in_dim(up_branch, start, block, 1)
        gate = jnp.dot(tokens, weight_cols, preferred_element_type=jnp.float32)
        tangent = jnp.dot(tokens, probe_cols, preferred_element_type=jnp.float32)
        sig = jax.nn.sigmoid(gate)
        second = sig * (1.0 - sig) * (2.0 + gate * (1.0 - 2.0 * sig))
        weighted = (cot_cols.astype(jnp.float32) * up_cols.astype(jnp.float32) * second * tangent / TOKENS).astype(jnp.bfloat16)

        def add_group(total, which):
            first = (which * group).astype(jnp.int32)
            rows = lax.dynamic_slice_in_dim(tokens, first, group, 0)
            terms = lax.dynamic_slice_in_dim(weighted, first, group, 0)
            partial_value = lax.dot_general(rows, terms, (((0,), (0,)), ((), ())), preferred_element_type=jnp.float32)
            rounded = lax.optimization_barrier(partial_value.astype(jnp.bfloat16))
            return total + rounded.astype(jnp.float32), None

        zeros = jnp.zeros((D, block), jnp.float32)
        total, unused = lax.scan(add_group, zeros, jnp.arange(N_FSDP, dtype=jnp.int32))
        return total

    pieces = lax.map(one_block, jnp.arange(count, dtype=jnp.int32))
    hvp = jnp.transpose(pieces, (1, 0, 2)).reshape(D, FF)
    hess_diag = probe.astype(jnp.float32) * hvp
    ema_next = 0.99 * hess_ema + 0.01 * hess_diag
    return hess_diag, ema_next
```

```python
import jax
import jax.numpy as jnp
from jax import lax
from jax.sharding import PartitionSpec as P


def body(tokens, cotangent, up_branch, gate_weight, probe, hess_ema):
    groups = lax.axis_size("fsdp")
    rows = gate_weight.shape[0]
    pieces = tokens.reshape(tokens.shape[0], groups, rows).transpose(1, 0, 2)
    pieces = lax.all_to_all(pieces, "fsdp", 0, 0, tiled=True)
    whole = lax.all_gather(pieces, "tp", axis=1, tiled=True).reshape(-1, rows)
    total_tokens = whole.shape[0]

    def summed(weight):
        part = jnp.dot(whole, weight, preferred_element_type=jnp.float32)
        return lax.psum_scatter(
            part.astype(jnp.bfloat16), "fsdp", scatter_dimension=0, tiled=True
        ).astype(jnp.float32)

    gate = summed(gate_weight)
    tangent = summed(probe)
    sig = jax.nn.sigmoid(gate)
    second = sig * (1.0 - sig) * (2.0 + gate * (1.0 - 2.0 * sig))
    weighted = (
        cotangent.astype(jnp.float32)
        * up_branch.astype(jnp.float32)
        * second
        * tangent
        / total_tokens
    ).astype(jnp.bfloat16)
    every = lax.all_gather(weighted, "fsdp", axis=0, tiled=True)
    hvp = lax.dot_general(
        whole, every, (((0,), (0,)), ((), ())), preferred_element_type=jnp.float32
    )
    hess_diag = probe.astype(jnp.float32) * hvp
    ema_next = 0.99 * hess_ema + 0.01 * hess_diag
    return (hess_diag, ema_next)


def solution(mesh):
    placed = (
        P(("fsdp", "tp"), None),
        P("fsdp", "tp"),
        P("fsdp", "tp"),
        P("fsdp", "tp"),
        P("fsdp", "tp"),
        P("fsdp", "tp"),
    )
    return jax.shard_map(
        body,
        mesh=mesh,
        in_specs=placed,
        out_specs=(P("fsdp", "tp"), P("fsdp", "tp")),
        check_vma=False,
    )
```

```python
import jax
import jax.numpy as jnp
from jax import lax
from jax.experimental import pallas as pl
from jax.experimental.pallas import tpu as pltpu
from jax.sharding import PartitionSpec as P

MESH = pl.DeviceIdType.MESH
TILE = 256


def pick(z, row):
    out = row[0]
    for index in range(1, len(row)):
        out = jnp.where(z == index, row[index], out)
    return out


def kernel(
    tokens, cotangent, up_branch, gate_weight, probe, hvp,
    weights, tok, toks2, tok_t, psend, precv, pown, wall, cot, up,
    own_sem, cu_sem, wl_sem, ws_sem, wr_sem, tr_sem, tx_sem, ty_sem, tu_sem, td_sem,
    ss_sem, sr_sem, ps_sem, pr_sem, vx_sem, vs_sem, vf_sem, rx_sem, rs_sem, rf_sem,
):
    f = lax.axis_index("fsdp")
    t = lax.axis_index("tp")
    x, c, z, y = f // 2, f % 2, t // 2, t % 2
    across = (2 * (1 - x) + c, t)
    sibling = (2 * x + 1 - c, t)
    beside = (f, 2 * z + 1 - y)
    above = (f, 2 * jnp.minimum(z + 1, 3) + y)
    below = (f, 2 * jnp.maximum(z - 1, 0) + y)
    rows, half = gate_weight.shape[0], 2 * gate_weight.shape[0]
    tiles = gate_weight.shape[1] // TILE
    total_tokens = 4 * cotangent.shape[0]
    part = 2 * tokens.shape[0]

    def remote(src, dst, send, recv, device):
        return pltpu.make_async_remote_copy(
            src_ref=src, dst_ref=dst, send_sem=send, recv_sem=recv,
            device_id=device, device_id_type=MESH,
        )

    def columns(index):
        return pl.ds(pl.multiple_of(index * TILE, TILE), TILE)

    own = pltpu.make_async_copy(
        tokens.at[:, pl.ds(pl.multiple_of(x * half, 128), half)], tok.at[x, z, y], own_sem
    )
    own.start()

    def local_weight(j, a):
        src = (gate_weight, probe)[a]
        return pltpu.make_async_copy(
            src.at[:, columns(j)], weights.at[j, a, c], wl_sem.at[j, a]
        )

    @pl.loop(0, tiles)
    def _(j):
        for a in range(2):
            local_weight(j, a).start()

    cot_copy = pltpu.make_async_copy(cotangent, cot, cu_sem.at[0])
    up_copy = pltpu.make_async_copy(up_branch, up, cu_sem.at[1])
    cot_copy.start()
    up_copy.start()

    barrier = pltpu.get_barrier_semaphore()
    for device in (across, sibling, beside):
        pl.semaphore_signal(barrier, inc=1, device_id=device, device_id_type=MESH)

    @pl.when(z < 3)
    def _():
        pl.semaphore_signal(barrier, inc=1, device_id=above, device_id_type=MESH)

    @pl.when(z > 0)
    def _():
        pl.semaphore_signal(barrier, inc=1, device_id=below, device_id_type=MESH)

    peers = 3 + jnp.minimum(z, 1) + jnp.minimum(3 - z, 1)
    pl.semaphore_wait(barrier, peers)

    def token_copy(xs, zs, sems, device):
        slot = tok.at[xs, zs, y]
        return remote(slot, slot, sems.at[xs, zs], tr_sem.at[xs, zs, y], device)

    def forward_up(xs, zs):
        @pl.when(z < 3)
        def _():
            token_copy(xs, zs, tu_sem, above).start()

    def forward_down(xs, zs):
        @pl.when(z > 0)
        def _():
            token_copy(xs, zs, td_sem, below).start()

    def token_wait(xs, zs, ys):
        slot = tok.at[xs, zs, ys]
        remote(slot, slot, ty_sem.at[xs, zs], tr_sem.at[xs, zs, ys], beside).wait_recv()

    to_across = remote(
        tokens.at[:, pl.ds(pl.multiple_of((1 - x) * half, 128), half)],
        tok.at[x, z, y], tx_sem, tr_sem.at[x, z, y], across,
    )
    to_across.start()
    own.wait()
    forward_up(x, z)
    forward_down(x, z)
    token_copy(x, z, ty_sem, beside).start()

    def sibling_weight(j, a):
        src = (gate_weight, probe)[a]
        return remote(
            src.at[:, columns(j)], weights.at[j, a, c], ws_sem.at[j, a], wr_sem.at[j, a], sibling
        )

    def arrived_weight(j, a):
        slot = weights.at[j, a, 1 - c]
        return remote(slot, slot, ws_sem.at[j, a], wr_sem.at[j, a], sibling)

    @pl.loop(0, tiles)
    def _(j):
        for a in range(2):
            sibling_weight(j, a).start()

    token_wait(1 - x, z, y)
    forward_up(1 - x, z)
    forward_down(1 - x, z)
    token_copy(1 - x, z, ty_sem, beside).start()

    def forward(d):
        @pl.when(z - d >= 0)
        def _():
            for xs in (x, 1 - x):
                token_wait(xs, z - d, y)
                forward_up(xs, z - d)
                token_copy(xs, z - d, ty_sem, beside).start()

        @pl.when(z + d <= 3)
        def _():
            for xs in (x, 1 - x):
                token_wait(xs, z + d, y)
                forward_down(xs, z + d)
                token_copy(xs, z + d, ty_sem, beside).start()

    def place(k):
        order = ((0, 1, 2, 3), (1, 0, 2, 3), (2, 1, 3, 0), (3, 2, 1, 0))
        return pick(z, [pick(k, line) for line in order])

    def partial_copy(zk, j):
        return remote(
            psend.at[zk, j], precv.at[zk, j], ps_sem.at[zk, j], pr_sem.at[zk, j], across
        )

    def sibling_tokens(xs, zk):
        return remote(
            tok.at[xs, zk, :, :, pl.ds(pl.multiple_of((1 - c) * rows, 128), rows)],
            toks2.at[xs, zk], ss_sem.at[xs, zk], sr_sem.at[xs, zk], sibling,
        )

    @pl.loop(0, 4)
    def _(k):
        zk = place(k)
        for xs in (x, 1 - x):
            token_wait(xs, zk, 1 - y)

        @pl.loop(0, tiles)
        def _(j):
            @pl.when(jnp.logical_and(k < 3, j == 1))
            def _():
                forward(k + 1)

            @pl.when(k == 0)
            def _():
                for a in range(2):
                    local_weight(j, a).wait()
                    arrived_weight(j, a).wait_recv()

            lhs = jnp.concatenate(
                [tok[1 - x, zk].reshape(part, half), tok[x, zk].reshape(part, half)], axis=0
            )
            for a in range(2):
                value = jnp.dot(
                    lhs[:, :rows], weights[j, a, 0], preferred_element_type=jnp.float32
                ) + jnp.dot(
                    lhs[:, rows:], weights[j, a, 1], preferred_element_type=jnp.float32
                )
                psend[zk, j, a] = value[:part].astype(jnp.bfloat16)
                pown[zk, j, a] = value[part:]
            partial_copy(zk, j).start()

        for xs in range(2):
            sibling_tokens(xs, zk).start()

    cot_copy.wait()
    up_copy.wait()

    def weighted_copy(xs, zk, j, send, recv, device):
        slot = wall.at[xs, c, zk, j]
        return remote(slot, slot, send.at[zk, j], recv.at[zk, j], device)

    @pl.loop(0, 4)
    def _(k):
        zk = place(k)

        @pl.loop(0, tiles)
        def _(j):
            partial_copy(zk, j).wait_recv()
            gate = pown[zk, j, 0] + precv[zk, j, 0].astype(jnp.float32)
            tangent = pown[zk, j, 1] + precv[zk, j, 1].astype(jnp.float32)
            sig = jax.nn.sigmoid(gate)
            second = sig * (1.0 - sig) * (2.0 + gate * (1.0 - 2.0 * sig))
            lines = pl.ds(pl.multiple_of(zk * part, part), part)
            wall[x, c, zk, j] = (
                cot[lines, columns(j)].astype(jnp.float32)
                * up[lines, columns(j)].astype(jnp.float32)
                * second
                * tangent
                * (1.0 / total_tokens)
            ).astype(jnp.bfloat16)
            weighted_copy(x, zk, j, vx_sem, rx_sem, across).start()
            weighted_copy(x, zk, j, vs_sem, rs_sem, sibling).start()

        mine = pl.ds(pl.multiple_of(c * rows, 128), rows)
        for xs in range(2):
            remote(
                toks2.at[xs, zk], toks2.at[xs, zk], ss_sem.at[xs, zk], sr_sem.at[xs, zk], sibling
            ).wait_recv()
        lines = [tok[xs, zk, :, :, mine].reshape(part, rows) for xs in range(2)]
        lines += [toks2[xs, zk].reshape(part, rows) for xs in range(2)]
        whole = jnp.concatenate(lines, axis=0).astype(jnp.float32)
        tok_t[k] = whole.T.astype(jnp.bfloat16)

    def arrived(xs, zk, j, recv):
        slot = wall.at[xs, 1 - c, zk, j]
        return remote(slot, slot, vs_sem.at[zk, j], recv.at[zk, j], sibling)

    def pass_on(k):
        zk = place(k)

        @pl.loop(0, tiles)
        def _(j):
            slot = wall.at[1 - x, c, zk, j]
            remote(slot, slot, vx_sem.at[zk, j], rx_sem.at[zk, j], across).wait_recv()
            weighted_copy(1 - x, zk, j, vf_sem, rf_sem, sibling).start()

    def backward(k):
        zk = place(k)

        @pl.loop(0, tiles)
        def _(j):
            arrived(x, zk, j, rs_sem).wait_recv()
            arrived(1 - x, zk, j, rf_sem).wait_recv()
            rhs = jnp.concatenate(
                [wall[0, c, zk, j], wall[1, c, zk, j], wall[0, 1 - c, zk, j], wall[1, 1 - c, zk, j]],
                axis=0,
            )
            value = jnp.dot(tok_t[k], rhs, preferred_element_type=jnp.float32)

            @pl.when(k == 0)
            def _():
                hvp[:, columns(j)] = value

            @pl.when(k > 0)
            def _():
                hvp[:, columns(j)] += value

    @pl.loop(0, 5)
    def _(k):
        @pl.when(k < 4)
        def _():
            pass_on(k)

        @pl.when(k > 0)
        def _():
            backward(k - 1)

    to_across.wait_send()

    @pl.loop(0, tiles)
    def _(j):
        for a in range(2):
            sibling_weight(j, a).wait_send()

    @pl.loop(0, 4)
    def _(zk):
        for xs in range(2):
            token_copy(xs, zk, ty_sem, beside).wait_send()
            sibling_tokens(xs, zk).wait_send()

            @pl.when(jnp.logical_and(z < 3, zk <= z))
            def _():
                token_copy(xs, zk, tu_sem, above).wait_send()

            @pl.when(jnp.logical_and(z > 0, zk >= z))
            def _():
                token_copy(xs, zk, td_sem, below).wait_send()

        @pl.loop(0, tiles)
        def _(j):
            partial_copy(zk, j).wait_send()
            weighted_copy(x, zk, j, vx_sem, rx_sem, across).wait_send()
            weighted_copy(x, zk, j, vs_sem, rs_sem, sibling).wait_send()
            weighted_copy(1 - x, zk, j, vf_sem, rf_sem, sibling).wait_send()


def small_body(tokens, cotangent, up_branch, gate_weight, probe, hess_ema):
    rows, width = gate_weight.shape
    lines = tokens.shape[0]
    part, tiles = 2 * lines, width // TILE
    bf16, f32, dma = jnp.bfloat16, jnp.float32, pltpu.SemaphoreType.DMA
    anywhere = pl.BlockSpec(memory_space=pl.ANY)
    grid = (4, tiles)
    hvp = pl.pallas_call(
        kernel,
        out_shape=jax.ShapeDtypeStruct((rows, width), f32),
        in_specs=[anywhere] * 5,
        out_specs=pl.BlockSpec(memory_space=pltpu.VMEM),
        scratch_shapes=[
            pltpu.VMEM((tiles, 2, 2, rows, TILE), bf16),
            pltpu.VMEM((2, 4, 2, lines, 2 * rows), bf16),
            pltpu.VMEM((2, 4, 2, lines, rows), bf16),
            pltpu.VMEM((4, rows, 4 * part), bf16),
            pltpu.VMEM((4, tiles, 2, part, TILE), bf16),
            pltpu.VMEM((4, tiles, 2, part, TILE), bf16),
            pltpu.VMEM((4, tiles, 2, part, TILE), f32),
            pltpu.VMEM((2, 2, 4, tiles, part, TILE), bf16),
            pltpu.VMEM(cotangent.shape, bf16),
            pltpu.VMEM(up_branch.shape, bf16),
            dma, dma((2,)), dma((tiles, 2)), dma((tiles, 2)), dma((tiles, 2)),
            dma((2, 4, 2)), dma, dma((2, 4)), dma((2, 4)), dma((2, 4)),
            dma((2, 4)), dma((2, 4)), dma(grid), dma(grid),
            dma(grid), dma(grid), dma(grid), dma(grid), dma(grid), dma(grid),
        ],
        compiler_params=pltpu.CompilerParams(
            collective_id=0, has_side_effects=True, vmem_limit_bytes=44 * 1024 * 1024
        ),
        cost_estimate=pl.CostEstimate(
            flops=7_000_000_000, bytes_accessed=12_000_000, transcendentals=500_000
        ),
    )(tokens, cotangent, up_branch, gate_weight, probe)
    hess_diag = probe.astype(f32) * hvp
    ema_next = 0.99 * hess_ema + 0.01 * hess_diag
    return (hess_diag, ema_next)


def body(tokens, cotangent, up_branch, gate_weight, probe, hess_ema):
    groups = lax.axis_size("fsdp")
    rows = gate_weight.shape[0]
    pieces = tokens.reshape(tokens.shape[0], groups, rows).transpose(1, 0, 2)
    pieces = lax.all_to_all(pieces, "fsdp", 0, 0, tiled=True)
    whole = lax.all_gather(pieces, "tp", axis=1, tiled=True).reshape(-1, rows)
    total_tokens = whole.shape[0]

    def summed(weight):
        part = jnp.dot(whole, weight, preferred_element_type=jnp.float32)
        return lax.psum_scatter(
            part.astype(jnp.bfloat16), "fsdp", scatter_dimension=0, tiled=True
        ).astype(jnp.float32)

    gate = summed(gate_weight)
    tangent = summed(probe)
    sig = jax.nn.sigmoid(gate)
    second = sig * (1.0 - sig) * (2.0 + gate * (1.0 - 2.0 * sig))
    weighted = (
        cotangent.astype(jnp.float32)
        * up_branch.astype(jnp.float32)
        * second
        * tangent
        / total_tokens
    ).astype(jnp.bfloat16)
    every = lax.all_gather(weighted, "fsdp", axis=0, tiled=True)
    hvp = lax.dot_general(
        whole, every, (((0,), (0,)), ((), ())), preferred_element_type=jnp.float32
    )
    hess_diag = probe.astype(jnp.float32) * hvp
    ema_next = 0.99 * hess_ema + 0.01 * hess_diag
    return (hess_diag, ema_next)


def solution(mesh):
    placed = (
        P(("fsdp", "tp"), None),
        P("fsdp", "tp"),
        P("fsdp", "tp"),
        P("fsdp", "tp"),
        P("fsdp", "tp"),
        P("fsdp", "tp"),
    )
    small = mesh.shape["fsdp"] == 4 and mesh.shape["tp"] == 8
    return jax.shard_map(
        small_body if small else body,
        mesh=mesh,
        in_specs=placed,
        out_specs=(P("fsdp", "tp"), P("fsdp", "tp")),
        check_vma=False,
    )
```

```python
import jax
import jax.numpy as jnp
from jax import lax
from jax.experimental import pallas as pl
from jax.experimental.pallas import tpu as pltpu
from jax.sharding import PartitionSpec as P

MESH = pl.DeviceIdType.MESH
TILE = 256


def pick(z, row):
    out = row[0]
    for index in range(1, len(row)):
        out = jnp.where(z == index, row[index], out)
    return out


def kernel(
    tokens, cotangent, up_branch, gate_weight, probe, hvp,
    weights, tok, toks2, tok_t, psend, precv, pown, wall, cot, up,
    own_sem, cu_sem, wl_sem, ws_sem, wr_sem, tr_sem, tx_sem, ty_sem, tu_sem, td_sem,
    ss_sem, sr_sem, ps_sem, pr_sem, vx_sem, vs_sem, vf_sem, rx_sem, rs_sem, rf_sem,
):
    f = lax.axis_index("fsdp")
    t = lax.axis_index("tp")
    x, c, z, y = f // 2, f % 2, t // 2, t % 2
    across = (2 * (1 - x) + c, t)
    sibling = (2 * x + 1 - c, t)
    beside = (f, 2 * z + 1 - y)
    above = (f, 2 * jnp.minimum(z + 1, 3) + y)
    below = (f, 2 * jnp.maximum(z - 1, 0) + y)
    rows, half = gate_weight.shape[0], 2 * gate_weight.shape[0]
    tiles = gate_weight.shape[1] // TILE
    total_tokens = 4 * cotangent.shape[0]
    part = 2 * tokens.shape[0]

    def remote(src, dst, send, recv, device):
        return pltpu.make_async_remote_copy(
            src_ref=src, dst_ref=dst, send_sem=send, recv_sem=recv,
            device_id=device, device_id_type=MESH,
        )

    def columns(index):
        return pl.ds(pl.multiple_of(index * TILE, TILE), TILE)

    own = pltpu.make_async_copy(
        tokens.at[:, pl.ds(pl.multiple_of(x * half, 128), half)], tok.at[x, z, y], own_sem
    )
    own.start()

    def local_weight(j, a):
        src = (gate_weight, probe)[a]
        return pltpu.make_async_copy(
            src.at[:, columns(j)], weights.at[j, a, c], wl_sem.at[j, a]
        )

    @pl.loop(0, tiles)
    def _(j):
        for a in range(2):
            local_weight(j, a).start()

    cot_copy = pltpu.make_async_copy(cotangent, cot, cu_sem.at[0])
    up_copy = pltpu.make_async_copy(up_branch, up, cu_sem.at[1])
    cot_copy.start()
    up_copy.start()

    barrier = pltpu.get_barrier_semaphore()
    for device in (across, sibling, beside):
        pl.semaphore_signal(barrier, inc=1, device_id=device, device_id_type=MESH)

    @pl.when(z < 3)
    def _():
        pl.semaphore_signal(barrier, inc=1, device_id=above, device_id_type=MESH)

    @pl.when(z > 0)
    def _():
        pl.semaphore_signal(barrier, inc=1, device_id=below, device_id_type=MESH)

    peers = 3 + jnp.minimum(z, 1) + jnp.minimum(3 - z, 1)
    pl.semaphore_wait(barrier, peers)

    def token_copy(xs, zs, sems, device):
        slot = tok.at[xs, zs, y]
        return remote(slot, slot, sems.at[xs, zs], tr_sem.at[xs, zs, y], device)

    def forward_up(xs, zs):
        @pl.when(z < 3)
        def _():
            token_copy(xs, zs, tu_sem, above).start()

    def forward_down(xs, zs):
        @pl.when(z > 0)
        def _():
            token_copy(xs, zs, td_sem, below).start()

    def token_wait(xs, zs, ys):
        slot = tok.at[xs, zs, ys]
        remote(slot, slot, ty_sem.at[xs, zs], tr_sem.at[xs, zs, ys], beside).wait_recv()

    to_across = remote(
        tokens.at[:, pl.ds(pl.multiple_of((1 - x) * half, 128), half)],
        tok.at[x, z, y], tx_sem, tr_sem.at[x, z, y], across,
    )
    to_across.start()
    own.wait()
    forward_up(x, z)
    forward_down(x, z)
    token_copy(x, z, ty_sem, beside).start()

    def sibling_weight(j, a):
        src = (gate_weight, probe)[a]
        return remote(
            src.at[:, columns(j)], weights.at[j, a, c], ws_sem.at[j, a], wr_sem.at[j, a], sibling
        )

    def arrived_weight(j, a):
        slot = weights.at[j, a, 1 - c]
        return remote(slot, slot, ws_sem.at[j, a], wr_sem.at[j, a], sibling)

    @pl.loop(0, tiles)
    def _(j):
        for a in range(2):
            sibling_weight(j, a).start()

    token_wait(1 - x, z, y)
    forward_up(1 - x, z)
    forward_down(1 - x, z)
    token_copy(1 - x, z, ty_sem, beside).start()

    def forward(d):
        @pl.when(z - d >= 0)
        def _():
            for xs in (x, 1 - x):
                token_wait(xs, z - d, y)
                forward_up(xs, z - d)
                token_copy(xs, z - d, ty_sem, beside).start()

        @pl.when(z + d <= 3)
        def _():
            for xs in (x, 1 - x):
                token_wait(xs, z + d, y)
                forward_down(xs, z + d)
                token_copy(xs, z + d, ty_sem, beside).start()

    def place(k):
        order = ((0, 1, 2, 3), (1, 0, 2, 3), (2, 1, 3, 0), (3, 2, 1, 0))
        return pick(z, [pick(k, line) for line in order])

    def partial_copy(zk, j):
        return remote(
            psend.at[zk, j], precv.at[zk, j], ps_sem.at[zk, j], pr_sem.at[zk, j], across
        )

    def sibling_tokens(xs, zk):
        return remote(
            tok.at[xs, zk, :, :, pl.ds(pl.multiple_of((1 - c) * rows, 128), rows)],
            toks2.at[xs, zk], ss_sem.at[xs, zk], sr_sem.at[xs, zk], sibling,
        )

    @pl.loop(0, 4)
    def _(k):
        zk = place(k)
        for xs in (x, 1 - x):
            token_wait(xs, zk, 1 - y)

        @pl.loop(0, tiles)
        def _(j):
            @pl.when(jnp.logical_and(k < 3, j == 1))
            def _():
                forward(k + 1)

            @pl.when(k == 0)
            def _():
                for a in range(2):
                    local_weight(j, a).wait()
                    arrived_weight(j, a).wait_recv()

            lhs = jnp.concatenate(
                [tok[1 - x, zk].reshape(part, half), tok[x, zk].reshape(part, half)], axis=0
            )
            for a in range(2):
                value = jnp.dot(
                    lhs[:, :rows], weights[j, a, 0], preferred_element_type=jnp.float32
                ) + jnp.dot(
                    lhs[:, rows:], weights[j, a, 1], preferred_element_type=jnp.float32
                )
                psend[zk, j, a] = value[:part].astype(jnp.bfloat16)
                pown[zk, j, a] = value[part:]
            partial_copy(zk, j).start()

        for xs in range(2):
            sibling_tokens(xs, zk).start()

    cot_copy.wait()
    up_copy.wait()

    def weighted_copy(xs, zk, j, send, recv, device):
        slot = wall.at[xs, c, zk, j]
        return remote(slot, slot, send.at[zk, j], recv.at[zk, j], device)

    @pl.loop(0, 4)
    def _(k):
        zk = place(k)

        @pl.loop(0, tiles)
        def _(j):
            partial_copy(zk, j).wait_recv()
            gate = pown[zk, j, 0] + precv[zk, j, 0].astype(jnp.float32)
            tangent = pown[zk, j, 1] + precv[zk, j, 1].astype(jnp.float32)
            sig = jax.nn.sigmoid(gate)
            second = sig * (1.0 - sig) * (2.0 + gate * (1.0 - 2.0 * sig))
            lines = pl.ds(pl.multiple_of(zk * part, part), part)
            wall[x, c, zk, j] = (
                cot[lines, columns(j)].astype(jnp.float32)
                * up[lines, columns(j)].astype(jnp.float32)
                * second
                * tangent
                * (1.0 / total_tokens)
            ).astype(jnp.bfloat16)
            weighted_copy(x, zk, j, vx_sem, rx_sem, across).start()
            weighted_copy(x, zk, j, vs_sem, rs_sem, sibling).start()

        mine = pl.ds(pl.multiple_of(c * rows, 128), rows)
        for xs in range(2):
            remote(
                toks2.at[xs, zk], toks2.at[xs, zk], ss_sem.at[xs, zk], sr_sem.at[xs, zk], sibling
            ).wait_recv()
        lines = [tok[xs, zk, :, :, mine].reshape(part, rows) for xs in range(2)]
        lines += [toks2[xs, zk].reshape(part, rows) for xs in range(2)]
        whole = jnp.concatenate(lines, axis=0).astype(jnp.float32)
        tok_t[k] = whole.T.astype(jnp.bfloat16)

    def arrived(xs, zk, j, recv):
        slot = wall.at[xs, 1 - c, zk, j]
        return remote(slot, slot, vs_sem.at[zk, j], recv.at[zk, j], sibling)

    def pass_on(k):
        zk = place(k)

        @pl.loop(0, tiles)
        def _(j):
            slot = wall.at[1 - x, c, zk, j]
            remote(slot, slot, vx_sem.at[zk, j], rx_sem.at[zk, j], across).wait_recv()
            weighted_copy(1 - x, zk, j, vf_sem, rf_sem, sibling).start()

    def backward(k):
        zk = place(k)

        @pl.loop(0, tiles)
        def _(j):
            arrived(x, zk, j, rs_sem).wait_recv()
            arrived(1 - x, zk, j, rf_sem).wait_recv()
            rhs = jnp.concatenate(
                [wall[0, c, zk, j], wall[1, c, zk, j], wall[0, 1 - c, zk, j], wall[1, 1 - c, zk, j]],
                axis=0,
            )
            value = jnp.dot(tok_t[k], rhs, preferred_element_type=jnp.float32)

            @pl.when(k == 0)
            def _():
                hvp[:, columns(j)] = value

            @pl.when(k > 0)
            def _():
                hvp[:, columns(j)] += value

    @pl.loop(0, 5)
    def _(k):
        @pl.when(k < 4)
        def _():
            pass_on(k)

        @pl.when(k > 0)
        def _():
            backward(k - 1)

    to_across.wait_send()

    @pl.loop(0, tiles)
    def _(j):
        for a in range(2):
            sibling_weight(j, a).wait_send()

    @pl.loop(0, 4)
    def _(zk):
        for xs in range(2):
            token_copy(xs, zk, ty_sem, beside).wait_send()
            sibling_tokens(xs, zk).wait_send()

            @pl.when(jnp.logical_and(z < 3, zk <= z))
            def _():
                token_copy(xs, zk, tu_sem, above).wait_send()

            @pl.when(jnp.logical_and(z > 0, zk >= z))
            def _():
                token_copy(xs, zk, td_sem, below).wait_send()

        @pl.loop(0, tiles)
        def _(j):
            partial_copy(zk, j).wait_send()
            weighted_copy(x, zk, j, vx_sem, rx_sem, across).wait_send()
            weighted_copy(x, zk, j, vs_sem, rs_sem, sibling).wait_send()
            weighted_copy(1 - x, zk, j, vf_sem, rf_sem, sibling).wait_send()


def small_body(tokens, cotangent, up_branch, gate_weight, probe, hess_ema):
    rows, width = gate_weight.shape
    lines = tokens.shape[0]
    part, tiles = 2 * lines, width // TILE
    bf16, f32, dma = jnp.bfloat16, jnp.float32, pltpu.SemaphoreType.DMA
    anywhere = pl.BlockSpec(memory_space=pltpu.HBM)
    grid = (4, tiles)
    hvp = pl.pallas_call(
        kernel,
        out_shape=pltpu.VMEM((rows, width), f32),
        in_specs=[anywhere] * 5,
        out_specs=pl.BlockSpec(memory_space=pltpu.VMEM),
        scratch_shapes=[
            pltpu.VMEM((tiles, 2, 2, rows, TILE), bf16),
            pltpu.VMEM((2, 4, 2, lines, 2 * rows), bf16),
            pltpu.VMEM((2, 4, 2, lines, rows), bf16),
            pltpu.VMEM((4, rows, 4 * part), bf16),
            pltpu.VMEM((4, tiles, 2, part, TILE), bf16),
            pltpu.VMEM((4, tiles, 2, part, TILE), bf16),
            pltpu.VMEM((4, tiles, 2, part, TILE), f32),
            pltpu.VMEM((2, 2, 4, tiles, part, TILE), bf16),
            pltpu.VMEM(cotangent.shape, bf16),
            pltpu.VMEM(up_branch.shape, bf16),
            dma, dma((2,)), dma((tiles, 2)), dma((tiles, 2)), dma((tiles, 2)),
            dma((2, 4, 2)), dma, dma((2, 4)), dma((2, 4)), dma((2, 4)),
            dma((2, 4)), dma((2, 4)), dma(grid), dma(grid),
            dma(grid), dma(grid), dma(grid), dma(grid), dma(grid), dma(grid),
        ],
        compiler_params=pltpu.CompilerParams(
            collective_id=0, has_side_effects=True, vmem_limit_bytes=44 * 1024 * 1024
        ),
        cost_estimate=pl.CostEstimate(
            flops=7_000_000_000, bytes_accessed=12_000_000, transcendentals=500_000
        ),
    )(*(
        pltpu.with_memory_space_constraint(operand, pltpu.HBM)
        for operand in (tokens, cotangent, up_branch, gate_weight, probe)
    ))
    hess_diag = probe.astype(f32) * hvp
    ema_next = 0.99 * hess_ema + 0.01 * hess_diag
    return (hess_diag, ema_next)


def body(tokens, cotangent, up_branch, gate_weight, probe, hess_ema):
    groups = lax.axis_size("fsdp")
    rows = gate_weight.shape[0]
    pieces = tokens.reshape(tokens.shape[0], groups, rows).transpose(1, 0, 2)
    pieces = lax.all_to_all(pieces, "fsdp", 0, 0, tiled=True)
    whole = lax.all_gather(pieces, "tp", axis=1, tiled=True).reshape(-1, rows)
    total_tokens = whole.shape[0]

    def summed(weight):
        part = jnp.dot(whole, weight, preferred_element_type=jnp.float32)
        return lax.psum_scatter(
            part.astype(jnp.bfloat16), "fsdp", scatter_dimension=0, tiled=True
        ).astype(jnp.float32)

    gate = summed(gate_weight)
    tangent = summed(probe)
    sig = jax.nn.sigmoid(gate)
    second = sig * (1.0 - sig) * (2.0 + gate * (1.0 - 2.0 * sig))
    weighted = (
        cotangent.astype(jnp.float32)
        * up_branch.astype(jnp.float32)
        * second
        * tangent
        / total_tokens
    ).astype(jnp.bfloat16)
    every = lax.all_gather(weighted, "fsdp", axis=0, tiled=True)
    hvp = lax.dot_general(
        whole, every, (((0,), (0,)), ((), ())), preferred_element_type=jnp.float32
    )
    hess_diag = probe.astype(jnp.float32) * hvp
    ema_next = 0.99 * hess_ema + 0.01 * hess_diag
    return (hess_diag, ema_next)


def solution(mesh):
    placed = (
        P(("fsdp", "tp"), None),
        P("fsdp", "tp"),
        P("fsdp", "tp"),
        P("fsdp", "tp"),
        P("fsdp", "tp"),
        P("fsdp", "tp"),
    )
    small = mesh.shape["fsdp"] == 4 and mesh.shape["tp"] == 8
    return jax.shard_map(
        small_body if small else body,
        mesh=mesh,
        in_specs=placed,
        out_specs=(P("fsdp", "tp"), P("fsdp", "tp")),
        check_vma=False,
    )
```

```python
import jax
import jax.numpy as jnp
from jax import lax
from jax.experimental import pallas as pl
from jax.experimental.pallas import tpu as pltpu
from jax.sharding import PartitionSpec as P

MESH = pl.DeviceIdType.MESH
TILE = 256


def pick(z, row):
    out = row[0]
    for index in range(1, len(row)):
        out = jnp.where(z == index, row[index], out)
    return out


def kernel(
    tokens, cotangent, up_branch, gate_weight, probe, hvp,
    weights, tok, toks2, tok_t, psend, precv, pown, wall, cot, up,
    own_sem, cu_sem, wl_sem, ws_sem, wr_sem, tr_sem, tx_sem, ty_sem, tu_sem, td_sem,
    ss_sem, sr_sem, ps_sem, pr_sem, vx_sem, vs_sem, vf_sem, rx_sem, rs_sem, rf_sem, fs_sem, fr_sem,
):
    f = lax.axis_index("fsdp")
    t = lax.axis_index("tp")
    x, c, z, y = f // 2, f % 2, t // 2, t % 2
    across = (2 * (1 - x) + c, t)
    sibling = (2 * x + 1 - c, t)
    beside = (f, 2 * z + 1 - y)
    above = (f, 2 * jnp.minimum(z + 1, 3) + y)
    below = (f, 2 * jnp.maximum(z - 1, 0) + y)
    rows, half = gate_weight.shape[0], 2 * gate_weight.shape[0]
    tiles = gate_weight.shape[1] // TILE
    total_tokens = 4 * cotangent.shape[0]
    part = 2 * tokens.shape[0]

    def remote(src, dst, send, recv, device):
        return pltpu.make_async_remote_copy(
            src_ref=src, dst_ref=dst, send_sem=send, recv_sem=recv,
            device_id=device, device_id_type=MESH,
        )

    def columns(index):
        return pl.ds(pl.multiple_of(index * TILE, TILE), TILE)

    own = pltpu.make_async_copy(
        tokens.at[:, pl.ds(pl.multiple_of(x * half, 128), half)], tok.at[x, z, y], own_sem
    )
    own.start()

    def local_weight(j, a):
        src = (gate_weight, probe)[a]
        return pltpu.make_async_copy(
            src.at[:, columns(j)], weights.at[j, a, c], wl_sem.at[j, a]
        )

    @pl.loop(0, tiles)
    def _(j):
        for a in range(2):
            local_weight(j, a).start()

    cot_copy = pltpu.make_async_copy(cotangent, cot, cu_sem.at[0])
    up_copy = pltpu.make_async_copy(up_branch, up, cu_sem.at[1])
    cot_copy.start()
    up_copy.start()

    barrier = pltpu.get_barrier_semaphore()
    for device in (across, sibling, beside):
        pl.semaphore_signal(barrier, inc=1, device_id=device, device_id_type=MESH)

    @pl.when(z < 3)
    def _():
        pl.semaphore_signal(barrier, inc=1, device_id=above, device_id_type=MESH)

    @pl.when(z > 0)
    def _():
        pl.semaphore_signal(barrier, inc=1, device_id=below, device_id_type=MESH)

    peers = 3 + jnp.minimum(z, 1) + jnp.minimum(3 - z, 1)
    pl.semaphore_wait(barrier, peers)

    def token_copy(xs, zs, sems, device):
        slot = tok.at[xs, zs, y]
        return remote(slot, slot, sems.at[xs, zs], tr_sem.at[xs, zs, y], device)

    def forward_up(xs, zs):
        @pl.when(z < 3)
        def _():
            token_copy(xs, zs, tu_sem, above).start()

    def forward_down(xs, zs):
        @pl.when(z > 0)
        def _():
            token_copy(xs, zs, td_sem, below).start()

    def token_wait(xs, zs, ys):
        slot = tok.at[xs, zs, ys]
        remote(slot, slot, ty_sem.at[xs, zs], tr_sem.at[xs, zs, ys], beside).wait_recv()

    to_across = remote(
        tokens.at[:, pl.ds(pl.multiple_of((1 - x) * half, 128), half)],
        tok.at[x, z, y], tx_sem, tr_sem.at[x, z, y], across,
    )
    to_across.start()

    def sibling_weight(j, a):
        src = (gate_weight, probe)[a]
        return remote(
            src.at[:, columns(j)], weights.at[j, a, c], ws_sem.at[j, a], wr_sem.at[j, a], sibling
        )

    def arrived_weight(j, a):
        slot = weights.at[j, a, 1 - c]
        return remote(slot, slot, ws_sem.at[j, a], wr_sem.at[j, a], sibling)

    @pl.loop(0, tiles)
    def _(j):
        for a in range(2):
            sibling_weight(j, a).start()

    own.wait()
    forward_up(x, z)
    forward_down(x, z)
    token_copy(x, z, ty_sem, beside).start()

    token_wait(1 - x, z, y)
    forward_up(1 - x, z)
    forward_down(1 - x, z)
    token_copy(1 - x, z, ty_sem, beside).start()

    def forward(d):
        @pl.when(z - d >= 0)
        def _():
            for xs in (x, 1 - x):
                token_wait(xs, z - d, y)
                forward_up(xs, z - d)
                token_copy(xs, z - d, ty_sem, beside).start()

        @pl.when(z + d <= 3)
        def _():
            for xs in (x, 1 - x):
                token_wait(xs, z + d, y)
                forward_down(xs, z + d)
                token_copy(xs, z + d, ty_sem, beside).start()

    def place(k):
        order = ((0, 1, 2, 3), (1, 0, 2, 3), (2, 1, 3, 0), (3, 2, 1, 0))
        return pick(z, [pick(k, line) for line in order])

    def partial_copy(zk, j):
        return remote(
            psend.at[zk, j], precv.at[zk, j], ps_sem.at[zk, j], pr_sem.at[zk, j], across
        )

    def sibling_tokens(xs, zk):
        return remote(
            tok.at[xs, zk, :, :, pl.ds(pl.multiple_of((1 - c) * rows, 128), rows)],
            toks2.at[xs, zk], ss_sem.at[xs, zk], sr_sem.at[xs, zk], sibling,
        )

    def product(lhs, j, a):
        return jnp.dot(
            lhs[:, :rows], weights[j, a, 0], preferred_element_type=jnp.float32
        ) + jnp.dot(lhs[:, rows:], weights[j, a, 1], preferred_element_type=jnp.float32)

    lines = part // 2

    def first_copy(ys, j):
        band = pl.ds(pl.multiple_of(ys * lines, lines), lines)
        return remote(
            psend.at[z, j, :, band], precv.at[z, j, :, band],
            fs_sem.at[ys, j], fr_sem.at[ys, j], across,
        )

    def first_half(ys, j):
        lhs = jnp.concatenate([tok[1 - x, z, ys], tok[x, z, ys]], axis=0)
        band = pl.ds(pl.multiple_of(ys * lines, lines), lines)
        for a in range(2):
            value = product(lhs, j, a)
            psend[z, j, a, band, :] = value[:lines].astype(jnp.bfloat16)
            pown[z, j, a, band, :] = value[lines:]
        first_copy(ys, j).start()

    @pl.loop(0, tiles + 2)
    def _(j):
        @pl.when(j < tiles)
        def _():
            for a in range(2):
                local_weight(j, a).wait()
                arrived_weight(j, a).wait_recv()
            first_half(y, j)

        @pl.when(j == 1)
        def _():
            forward(1)
            for xs in (x, 1 - x):
                token_wait(xs, z, 1 - y)

        @pl.when(j >= 2)
        def _():
            first_half(1 - y, j - 2)

    for xs in range(2):
        sibling_tokens(xs, z).start()

    @pl.loop(1, 4)
    def _(k):
        zk = place(k)

        for xs in (x, 1 - x):
            token_wait(xs, zk, 1 - y)

        @pl.loop(0, tiles)
        def _(j):
            @pl.when(jnp.logical_and(k < 3, j == 1))
            def _():
                forward(k + 1)

            lhs = jnp.concatenate(
                [tok[1 - x, zk].reshape(part, half), tok[x, zk].reshape(part, half)], axis=0
            )
            for a in range(2):
                value = product(lhs, j, a)
                psend[zk, j, a] = value[:part].astype(jnp.bfloat16)
                pown[zk, j, a] = value[part:]
            partial_copy(zk, j).start()

        for xs in range(2):
            sibling_tokens(xs, zk).start()

    cot_copy.wait()
    up_copy.wait()

    def weighted_copy(xs, zk, j, send, recv, device):
        slot = wall.at[xs, c, zk, j]
        return remote(slot, slot, send.at[zk, j], recv.at[zk, j], device)

    @pl.loop(0, 4)
    def _(k):
        zk = place(k)

        @pl.loop(0, tiles)
        def _(j):
            @pl.when(k == 0)
            def _():
                for ys in range(2):
                    first_copy(ys, j).wait_recv()

            @pl.when(k > 0)
            def _():
                partial_copy(zk, j).wait_recv()

            gate = pown[zk, j, 0] + precv[zk, j, 0].astype(jnp.float32)
            tangent = pown[zk, j, 1] + precv[zk, j, 1].astype(jnp.float32)
            sig = jax.nn.sigmoid(gate)
            second = sig * (1.0 - sig) * (2.0 + gate * (1.0 - 2.0 * sig))
            lines = pl.ds(pl.multiple_of(zk * part, part), part)
            wall[x, c, zk, j] = (
                cot[lines, columns(j)].astype(jnp.float32)
                * up[lines, columns(j)].astype(jnp.float32)
                * second
                * tangent
                * (1.0 / total_tokens)
            ).astype(jnp.bfloat16)
            weighted_copy(x, zk, j, vx_sem, rx_sem, across).start()
            weighted_copy(x, zk, j, vs_sem, rs_sem, sibling).start()

        mine = pl.ds(pl.multiple_of(c * rows, 128), rows)
        for xs in range(2):
            remote(
                toks2.at[xs, zk], toks2.at[xs, zk], ss_sem.at[xs, zk], sr_sem.at[xs, zk], sibling
            ).wait_recv()
        lines = [tok[xs, zk, :, :, mine].reshape(part, rows) for xs in range(2)]
        lines += [toks2[xs, zk].reshape(part, rows) for xs in range(2)]
        whole = jnp.concatenate(lines, axis=0).astype(jnp.float32)
        tok_t[k] = whole.T.astype(jnp.bfloat16)

    def arrived(xs, zk, j, recv):
        slot = wall.at[xs, 1 - c, zk, j]
        return remote(slot, slot, vs_sem.at[zk, j], recv.at[zk, j], sibling)

    def pass_on(k, j):
        zk = place(k)
        slot = wall.at[1 - x, c, zk, j]
        remote(slot, slot, vx_sem.at[zk, j], rx_sem.at[zk, j], across).wait_recv()
        weighted_copy(1 - x, zk, j, vf_sem, rf_sem, sibling).start()

    def backward(k, j):
        zk = place(k)
        arrived(x, zk, j, rs_sem).wait_recv()
        arrived(1 - x, zk, j, rf_sem).wait_recv()
        rhs = jnp.concatenate(
            [wall[0, c, zk, j], wall[1, c, zk, j], wall[0, 1 - c, zk, j], wall[1, 1 - c, zk, j]],
            axis=0,
        )
        value = jnp.dot(tok_t[k], rhs, preferred_element_type=jnp.float32)

        @pl.when(k == 0)
        def _():
            hvp[:, columns(j)] = value

        @pl.when(k > 0)
        def _():
            hvp[:, columns(j)] += value

        @pl.when(k == 0)
        def _():
            for ys in range(2):
                first_copy(ys, j).wait_send()

        @pl.when(k > 0)
        def _():
            partial_copy(zk, j).wait_send()

        weighted_copy(x, zk, j, vx_sem, rx_sem, across).wait_send()
        weighted_copy(x, zk, j, vs_sem, rs_sem, sibling).wait_send()
        weighted_copy(1 - x, zk, j, vf_sem, rf_sem, sibling).wait_send()

    to_across.wait_send()

    @pl.loop(0, tiles)
    def _(j):
        for a in range(2):
            sibling_weight(j, a).wait_send()

    @pl.loop(0, 4)
    def _(zk):
        for xs in range(2):
            token_copy(xs, zk, ty_sem, beside).wait_send()
            sibling_tokens(xs, zk).wait_send()

            @pl.when(jnp.logical_and(z < 3, zk <= z))
            def _():
                token_copy(xs, zk, tu_sem, above).wait_send()

            @pl.when(jnp.logical_and(z > 0, zk >= z))
            def _():
                token_copy(xs, zk, td_sem, below).wait_send()

    lag = 2

    @pl.loop(0, 4 * tiles + lag)
    def _(u):
        @pl.when(u < 4 * tiles)
        def _():
            pass_on(u // tiles, u % tiles)

        @pl.when(u >= lag)
        def _():
            backward((u - lag) // tiles, (u - lag) % tiles)


def small_body(tokens, cotangent, up_branch, gate_weight, probe, hess_ema):
    rows, width = gate_weight.shape
    lines = tokens.shape[0]
    part, tiles = 2 * lines, width // TILE
    bf16, f32, dma = jnp.bfloat16, jnp.float32, pltpu.SemaphoreType.DMA
    anywhere = pl.BlockSpec(memory_space=pltpu.HBM)
    grid = (4, tiles)
    hvp = pl.pallas_call(
        kernel,
        out_shape=pltpu.VMEM((rows, width), f32),
        in_specs=[anywhere] * 5,
        out_specs=pl.BlockSpec(memory_space=pltpu.VMEM),
        scratch_shapes=[
            pltpu.VMEM((tiles, 2, 2, rows, TILE), bf16),
            pltpu.VMEM((2, 4, 2, lines, 2 * rows), bf16),
            pltpu.VMEM((2, 4, 2, lines, rows), bf16),
            pltpu.VMEM((4, rows, 4 * part), bf16),
            pltpu.VMEM((4, tiles, 2, part, TILE), bf16),
            pltpu.VMEM((4, tiles, 2, part, TILE), bf16),
            pltpu.VMEM((4, tiles, 2, part, TILE), f32),
            pltpu.VMEM((2, 2, 4, tiles, part, TILE), bf16),
            pltpu.VMEM(cotangent.shape, bf16),
            pltpu.VMEM(up_branch.shape, bf16),
            dma, dma((2,)), dma((tiles, 2)), dma((tiles, 2)), dma((tiles, 2)),
            dma((2, 4, 2)), dma, dma((2, 4)), dma((2, 4)), dma((2, 4)),
            dma((2, 4)), dma((2, 4)), dma(grid), dma(grid),
            dma(grid), dma(grid), dma(grid), dma(grid), dma(grid), dma(grid),
            dma((2, tiles)), dma((2, tiles)),
        ],
        compiler_params=pltpu.CompilerParams(
            collective_id=0, has_side_effects=True, vmem_limit_bytes=44 * 1024 * 1024
        ),
        cost_estimate=pl.CostEstimate(
            flops=7_000_000_000, bytes_accessed=12_000_000, transcendentals=500_000
        ),
    )(*(
        pltpu.with_memory_space_constraint(operand, pltpu.HBM)
        for operand in (tokens, cotangent, up_branch, gate_weight, probe)
    ))
    hess_diag = probe.astype(f32) * hvp
    ema_next = 0.99 * hess_ema + 0.01 * hess_diag
    return (hess_diag, ema_next)


def body(tokens, cotangent, up_branch, gate_weight, probe, hess_ema):
    groups = lax.axis_size("fsdp")
    rows = gate_weight.shape[0]
    pieces = tokens.reshape(tokens.shape[0], groups, rows).transpose(1, 0, 2)
    pieces = lax.all_to_all(pieces, "fsdp", 0, 0, tiled=True)
    whole = lax.all_gather(pieces, "tp", axis=1, tiled=True).reshape(-1, rows)
    total_tokens = whole.shape[0]

    def summed(weight):
        part = jnp.dot(whole, weight, preferred_element_type=jnp.float32)
        return lax.psum_scatter(
            part.astype(jnp.bfloat16), "fsdp", scatter_dimension=0, tiled=True
        ).astype(jnp.float32)

    gate = summed(gate_weight)
    tangent = summed(probe)
    sig = jax.nn.sigmoid(gate)
    second = sig * (1.0 - sig) * (2.0 + gate * (1.0 - 2.0 * sig))
    weighted = (
        cotangent.astype(jnp.float32)
        * up_branch.astype(jnp.float32)
        * second
        * tangent
        / total_tokens
    ).astype(jnp.bfloat16)
    every = lax.all_gather(weighted, "fsdp", axis=0, tiled=True)
    hvp = lax.dot_general(
        whole, every, (((0,), (0,)), ((), ())), preferred_element_type=jnp.float32
    )
    hess_diag = probe.astype(jnp.float32) * hvp
    ema_next = 0.99 * hess_ema + 0.01 * hess_diag
    return (hess_diag, ema_next)


def solution(mesh):
    placed = (
        P(("fsdp", "tp"), None),
        P("fsdp", "tp"),
        P("fsdp", "tp"),
        P("fsdp", "tp"),
        P("fsdp", "tp"),
        P("fsdp", "tp"),
    )
    small = mesh.shape["fsdp"] == 4 and mesh.shape["tp"] == 8
    return jax.shard_map(
        small_body if small else body,
        mesh=mesh,
        in_specs=placed,
        out_specs=(P("fsdp", "tp"), P("fsdp", "tp")),
        check_vma=False,
    )
```

```python
import jax
import jax.numpy as jnp
from jax import lax
from jax.experimental import pallas as pl
from jax.experimental.pallas import tpu as pltpu
from jax.sharding import PartitionSpec as P

MESH = pl.DeviceIdType.MESH
TILE = 256


def pick(z, row):
    out = row[0]
    for index in range(1, len(row)):
        out = jnp.where(z == index, row[index], out)
    return out


def kernel(
    tokens, cotangent, up_branch, gate_weight, probe, hvp,
    weights, tok, toks2, tok_t, psend, precv, pown, wall, cot, up,
    own_sem, cu_sem, wl_sem, ws_sem, wr_sem, tr_sem, tx_sem, ty_sem, tu_sem, td_sem,
    ss_sem, sr_sem, ps_sem, pr_sem, vx_sem, vs_sem, vf_sem, rx_sem, rs_sem, rf_sem, fs_sem, fr_sem,
):
    f = lax.axis_index("fsdp")
    t = lax.axis_index("tp")
    x, c, z, y = f // 2, f % 2, t // 2, t % 2
    across = (2 * (1 - x) + c, t)
    sibling = (2 * x + 1 - c, t)
    beside = (f, 2 * z + 1 - y)
    above = (f, 2 * jnp.minimum(z + 1, 3) + y)
    below = (f, 2 * jnp.maximum(z - 1, 0) + y)
    rows, half = gate_weight.shape[0], 2 * gate_weight.shape[0]
    tiles = gate_weight.shape[1] // TILE
    total_tokens = 4 * cotangent.shape[0]
    part = 2 * tokens.shape[0]

    def remote(src, dst, send, recv, device):
        return pltpu.make_async_remote_copy(
            src_ref=src, dst_ref=dst, send_sem=send, recv_sem=recv,
            device_id=device, device_id_type=MESH,
        )

    def columns(index):
        return pl.ds(pl.multiple_of(index * TILE, TILE), TILE)

    own = pltpu.make_async_copy(
        tokens.at[:, pl.ds(pl.multiple_of(x * half, 128), half)], tok.at[x, z, y], own_sem
    )
    own.start()

    def local_weight(j, a):
        src = (gate_weight, probe)[a]
        return pltpu.make_async_copy(
            src.at[:, columns(j)], weights.at[j, a, c], wl_sem.at[j, a]
        )

    @pl.loop(0, tiles)
    def _(j):
        for a in range(2):
            local_weight(j, a).start()

    cot_copy = pltpu.make_async_copy(cotangent, cot, cu_sem.at[0])
    up_copy = pltpu.make_async_copy(up_branch, up, cu_sem.at[1])
    cot_copy.start()
    up_copy.start()

    barrier = pltpu.get_barrier_semaphore()
    for device in (across, sibling, beside):
        pl.semaphore_signal(barrier, inc=1, device_id=device, device_id_type=MESH)

    @pl.when(z < 3)
    def _():
        pl.semaphore_signal(barrier, inc=1, device_id=above, device_id_type=MESH)

    @pl.when(z > 0)
    def _():
        pl.semaphore_signal(barrier, inc=1, device_id=below, device_id_type=MESH)

    peers = 3 + jnp.minimum(z, 1) + jnp.minimum(3 - z, 1)
    pl.semaphore_wait(barrier, peers)

    def token_copy(xs, zs, sems, device):
        slot = tok.at[xs, zs, y]
        return remote(slot, slot, sems.at[xs, zs], tr_sem.at[xs, zs, y], device)

    def forward_up(xs, zs):
        @pl.when(z < 3)
        def _():
            token_copy(xs, zs, tu_sem, above).start()

    def forward_down(xs, zs):
        @pl.when(z > 0)
        def _():
            token_copy(xs, zs, td_sem, below).start()

    def token_wait(xs, zs, ys):
        slot = tok.at[xs, zs, ys]
        remote(slot, slot, ty_sem.at[xs, zs], tr_sem.at[xs, zs, ys], beside).wait_recv()

    to_across = remote(
        tokens.at[:, pl.ds(pl.multiple_of((1 - x) * half, 128), half)],
        tok.at[x, z, y], tx_sem, tr_sem.at[x, z, y], across,
    )
    to_across.start()

    def sibling_weight(j, a):
        src = (gate_weight, probe)[a]
        return remote(
            src.at[:, columns(j)], weights.at[j, a, c], ws_sem.at[j, a], wr_sem.at[j, a], sibling
        )

    def arrived_weight(j, a):
        slot = weights.at[j, a, 1 - c]
        return remote(slot, slot, ws_sem.at[j, a], wr_sem.at[j, a], sibling)

    @pl.loop(0, tiles)
    def _(j):
        for a in range(2):
            sibling_weight(j, a).start()

    own.wait()
    forward_up(x, z)
    forward_down(x, z)
    token_copy(x, z, ty_sem, beside).start()

    token_wait(1 - x, z, y)
    forward_up(1 - x, z)
    forward_down(1 - x, z)
    token_copy(1 - x, z, ty_sem, beside).start()

    def forward(d):
        @pl.when(z - d >= 0)
        def _():
            for xs in (x, 1 - x):
                token_wait(xs, z - d, y)
                forward_up(xs, z - d)
                token_copy(xs, z - d, ty_sem, beside).start()

        @pl.when(z + d <= 3)
        def _():
            for xs in (x, 1 - x):
                token_wait(xs, z + d, y)
                forward_down(xs, z + d)
                token_copy(xs, z + d, ty_sem, beside).start()

    def place(k):
        order = ((0, 1, 2, 3), (1, 0, 2, 3), (2, 1, 3, 0), (3, 2, 1, 0))
        return pick(z, [pick(k, line) for line in order])

    def partial_copy(zk, j):
        return remote(
            psend.at[zk, j], precv.at[zk, j], ps_sem.at[zk, j], pr_sem.at[zk, j], across
        )

    def sibling_tokens(xs, zk):
        return remote(
            tok.at[xs, zk, :, :, pl.ds(pl.multiple_of((1 - c) * rows, 128), rows)],
            toks2.at[xs, zk], ss_sem.at[xs, zk], sr_sem.at[xs, zk], sibling,
        )

    def product(lhs, j, a):
        return jnp.dot(
            lhs[:, :rows], weights[j, a, 0], preferred_element_type=jnp.float32
        ) + jnp.dot(lhs[:, rows:], weights[j, a, 1], preferred_element_type=jnp.float32)

    lines = part // 2

    def first_copy(ys, j):
        band = pl.ds(pl.multiple_of(ys * lines, lines), lines)
        return remote(
            psend.at[z, j, :, band], precv.at[z, j, :, band],
            fs_sem.at[ys, j], fr_sem.at[ys, j], across,
        )

    def first_half(ys, j):
        lhs = jnp.concatenate([tok[1 - x, z, ys], tok[x, z, ys]], axis=0)
        band = pl.ds(pl.multiple_of(ys * lines, lines), lines)
        for a in range(2):
            value = product(lhs, j, a)
            psend[z, j, a, band, :] = value[:lines].astype(jnp.bfloat16)
            pown[z, j, a, band, :] = value[lines:]
        first_copy(ys, j).start()

    @pl.loop(0, tiles + 2)
    def _(j):
        @pl.when(j < tiles)
        def _():
            for a in range(2):
                local_weight(j, a).wait()
                arrived_weight(j, a).wait_recv()
            first_half(y, j)

        @pl.when(j == 1)
        def _():
            forward(1)
            for xs in (x, 1 - x):
                token_wait(xs, z, 1 - y)

        @pl.when(j >= 2)
        def _():
            first_half(1 - y, j - 2)

    for xs in range(2):
        sibling_tokens(xs, z).start()

    @pl.loop(1, 4)
    def _(k):
        zk = place(k)

        for xs in (x, 1 - x):
            token_wait(xs, zk, 1 - y)

        @pl.loop(0, tiles)
        def _(j):
            @pl.when(jnp.logical_and(k < 3, j == 1))
            def _():
                forward(k + 1)

            lhs = jnp.concatenate(
                [tok[1 - x, zk].reshape(part, half), tok[x, zk].reshape(part, half)], axis=0
            )
            for a in range(2):
                value = product(lhs, j, a)
                psend[zk, j, a] = value[:part].astype(jnp.bfloat16)
                pown[zk, j, a] = value[part:]
            partial_copy(zk, j).start()

        for xs in range(2):
            sibling_tokens(xs, zk).start()

    cot_copy.wait()
    up_copy.wait()

    def weighted_copy(xs, zk, j, send, recv, device):
        slot = wall.at[xs, c, zk, j]
        return remote(slot, slot, send.at[zk, j], recv.at[zk, j], device)

    @pl.loop(0, 4)
    def _(k):
        zk = place(k)

        @pl.loop(0, tiles)
        def _(j):
            @pl.when(k == 0)
            def _():
                for ys in range(2):
                    first_copy(ys, j).wait_recv()

            @pl.when(k > 0)
            def _():
                partial_copy(zk, j).wait_recv()

            gate = pown[zk, j, 0] + precv[zk, j, 0].astype(jnp.float32)
            tangent = pown[zk, j, 1] + precv[zk, j, 1].astype(jnp.float32)
            sig = jax.nn.sigmoid(gate)
            second = sig * (1.0 - sig) * (2.0 + gate * (1.0 - 2.0 * sig))
            lines = pl.ds(pl.multiple_of(zk * part, part), part)
            wall[x, c, zk, j] = (
                cot[lines, columns(j)].astype(jnp.float32)
                * up[lines, columns(j)].astype(jnp.float32)
                * second
                * tangent
                * (1.0 / total_tokens)
            ).astype(jnp.bfloat16)
            weighted_copy(x, zk, j, vx_sem, rx_sem, across).start()
            weighted_copy(x, zk, j, vs_sem, rs_sem, sibling).start()

        mine = pl.ds(pl.multiple_of(c * rows, 128), rows)
        for xs in range(2):
            remote(
                toks2.at[xs, zk], toks2.at[xs, zk], ss_sem.at[xs, zk], sr_sem.at[xs, zk], sibling
            ).wait_recv()
        lines = [tok[xs, zk, :, :, mine].reshape(part, rows) for xs in range(2)]
        lines += [toks2[xs, zk].reshape(part, rows) for xs in range(2)]
        whole = jnp.concatenate(lines, axis=0).astype(jnp.float32)
        tok_t[k] = whole.T.astype(jnp.bfloat16)

    def arrived(xs, zk, j, recv):
        slot = wall.at[xs, 1 - c, zk, j]
        return remote(slot, slot, vs_sem.at[zk, j], recv.at[zk, j], sibling)

    def pass_on(k, j):
        zk = place(k)
        slot = wall.at[1 - x, c, zk, j]
        remote(slot, slot, vx_sem.at[zk, j], rx_sem.at[zk, j], across).wait_recv()
        weighted_copy(1 - x, zk, j, vf_sem, rf_sem, sibling).start()

    def backward(k, j):
        zk = place(k)
        arrived(x, zk, j, rs_sem).wait_recv()
        arrived(1 - x, zk, j, rf_sem).wait_recv()
        rhs = jnp.concatenate(
            [wall[0, c, zk, j], wall[1, c, zk, j], wall[0, 1 - c, zk, j], wall[1, 1 - c, zk, j]],
            axis=0,
        )
        value = jnp.dot(tok_t[k], rhs, preferred_element_type=jnp.float32)

        @pl.when(k == 0)
        def _():
            hvp[:, columns(j)] = value

        @pl.when(k > 0)
        def _():
            hvp[:, columns(j)] += value

        @pl.when(k == 0)
        def _():
            for ys in range(2):
                first_copy(ys, j).wait_send()

        @pl.when(k > 0)
        def _():
            partial_copy(zk, j).wait_send()

        weighted_copy(x, zk, j, vx_sem, rx_sem, across).wait_send()
        weighted_copy(x, zk, j, vs_sem, rs_sem, sibling).wait_send()
        weighted_copy(1 - x, zk, j, vf_sem, rf_sem, sibling).wait_send()

    to_across.wait_send()

    @pl.loop(0, tiles)
    def _(j):
        for a in range(2):
            sibling_weight(j, a).wait_send()

    @pl.loop(0, 4)
    def _(zk):
        for xs in range(2):
            token_copy(xs, zk, ty_sem, beside).wait_send()
            sibling_tokens(xs, zk).wait_send()

            @pl.when(jnp.logical_and(z < 3, zk <= z))
            def _():
                token_copy(xs, zk, tu_sem, above).wait_send()

            @pl.when(jnp.logical_and(z > 0, zk >= z))
            def _():
                token_copy(xs, zk, td_sem, below).wait_send()

    lag = 3

    @pl.loop(0, 4 * tiles + lag)
    def _(u):
        @pl.when(u < 4 * tiles)
        def _():
            pass_on(u // tiles, u % tiles)

        @pl.when(u >= lag)
        def _():
            backward((u - lag) // tiles, (u - lag) % tiles)


def small_body(tokens, cotangent, up_branch, gate_weight, probe, hess_ema):
    rows, width = gate_weight.shape
    lines = tokens.shape[0]
    part, tiles = 2 * lines, width // TILE
    bf16, f32, dma = jnp.bfloat16, jnp.float32, pltpu.SemaphoreType.DMA
    anywhere = pl.BlockSpec(memory_space=pltpu.HBM)
    grid = (4, tiles)
    hvp = pl.pallas_call(
        kernel,
        out_shape=pltpu.VMEM((rows, width), f32),
        in_specs=[anywhere] * 5,
        out_specs=pl.BlockSpec(memory_space=pltpu.VMEM),
        scratch_shapes=[
            pltpu.VMEM((tiles, 2, 2, rows, TILE), bf16),
            pltpu.VMEM((2, 4, 2, lines, 2 * rows), bf16),
            pltpu.VMEM((2, 4, 2, lines, rows), bf16),
            pltpu.VMEM((4, rows, 4 * part), bf16),
            pltpu.VMEM((4, tiles, 2, part, TILE), bf16),
            pltpu.VMEM((4, tiles, 2, part, TILE), bf16),
            pltpu.VMEM((4, tiles, 2, part, TILE), f32),
            pltpu.VMEM((2, 2, 4, tiles, part, TILE), bf16),
            pltpu.VMEM(cotangent.shape, bf16),
            pltpu.VMEM(up_branch.shape, bf16),
            dma, dma((2,)), dma((tiles, 2)), dma((tiles, 2)), dma((tiles, 2)),
            dma((2, 4, 2)), dma, dma((2, 4)), dma((2, 4)), dma((2, 4)),
            dma((2, 4)), dma((2, 4)), dma(grid), dma(grid),
            dma(grid), dma(grid), dma(grid), dma(grid), dma(grid), dma(grid),
            dma((2, tiles)), dma((2, tiles)),
        ],
        compiler_params=pltpu.CompilerParams(
            collective_id=0, has_side_effects=True, vmem_limit_bytes=44 * 1024 * 1024
        ),
        cost_estimate=pl.CostEstimate(
            flops=7_000_000_000, bytes_accessed=12_000_000, transcendentals=500_000
        ),
    )(*(
        pltpu.with_memory_space_constraint(operand, pltpu.HBM)
        for operand in (tokens, cotangent, up_branch, gate_weight, probe)
    ))
    hess_diag = probe.astype(f32) * hvp
    ema_next = 0.99 * hess_ema + 0.01 * hess_diag
    return (hess_diag, ema_next)


def body(tokens, cotangent, up_branch, gate_weight, probe, hess_ema):
    groups = lax.axis_size("fsdp")
    rows = gate_weight.shape[0]
    pieces = tokens.reshape(tokens.shape[0], groups, rows).transpose(1, 0, 2)
    pieces = lax.all_to_all(pieces, "fsdp", 0, 0, tiled=True)
    whole = lax.all_gather(pieces, "tp", axis=1, tiled=True).reshape(-1, rows)
    total_tokens = whole.shape[0]

    def summed(weight):
        part = jnp.dot(whole, weight, preferred_element_type=jnp.float32)
        return lax.psum_scatter(
            part.astype(jnp.bfloat16), "fsdp", scatter_dimension=0, tiled=True
        ).astype(jnp.float32)

    gate = summed(gate_weight)
    tangent = summed(probe)
    sig = jax.nn.sigmoid(gate)
    second = sig * (1.0 - sig) * (2.0 + gate * (1.0 - 2.0 * sig))
    weighted = (
        cotangent.astype(jnp.float32)
        * up_branch.astype(jnp.float32)
        * second
        * tangent
        / total_tokens
    ).astype(jnp.bfloat16)
    every = lax.all_gather(weighted, "fsdp", axis=0, tiled=True)
    hvp = lax.dot_general(
        whole, every, (((0,), (0,)), ((), ())), preferred_element_type=jnp.float32
    )
    hess_diag = probe.astype(jnp.float32) * hvp
    ema_next = 0.99 * hess_ema + 0.01 * hess_diag
    return (hess_diag, ema_next)


def solution(mesh):
    placed = (
        P(("fsdp", "tp"), None),
        P("fsdp", "tp"),
        P("fsdp", "tp"),
        P("fsdp", "tp"),
        P("fsdp", "tp"),
        P("fsdp", "tp"),
    )
    small = mesh.shape["fsdp"] == 4 and mesh.shape["tp"] == 8
    return jax.shard_map(
        small_body if small else body,
        mesh=mesh,
        in_specs=placed,
        out_specs=(P("fsdp", "tp"), P("fsdp", "tp")),
        check_vma=False,
    )
```

```python
import jax
import jax.numpy as jnp
from jax import lax
from jax.experimental import pallas as pl
from jax.experimental.pallas import tpu as pltpu
from jax.sharding import PartitionSpec as P

MESH = pl.DeviceIdType.MESH
TILE = 256


def pick(z, row):
    out = row[0]
    for index in range(1, len(row)):
        out = jnp.where(z == index, row[index], out)
    return out


def kernel(
    tokens, cotangent, up_branch, gate_weight, probe, hvp,
    weights, tok, toks2, tok_t, psend, precv, pown, wall, cot, up,
    own_sem, cu_sem, wl_sem, ws_sem, wr_sem, tr_sem, tx_sem, ty_sem, tu_sem, td_sem,
    ss_sem, sr_sem, ps_sem, pr_sem, vx_sem, vs_sem, vf_sem, rx_sem, rs_sem, rf_sem, fs_sem, fr_sem,
):
    f = lax.axis_index("fsdp")
    t = lax.axis_index("tp")
    x, c, z, y = f // 2, f % 2, t // 2, t % 2
    across = (2 * (1 - x) + c, t)
    sibling = (2 * x + 1 - c, t)
    beside = (f, 2 * z + 1 - y)
    above = (f, 2 * jnp.minimum(z + 1, 3) + y)
    below = (f, 2 * jnp.maximum(z - 1, 0) + y)
    rows, half = gate_weight.shape[0], 2 * gate_weight.shape[0]
    tiles = gate_weight.shape[1] // TILE
    total_tokens = 4 * cotangent.shape[0]
    part = 2 * tokens.shape[0]

    def remote(src, dst, send, recv, device):
        return pltpu.make_async_remote_copy(
            src_ref=src, dst_ref=dst, send_sem=send, recv_sem=recv,
            device_id=device, device_id_type=MESH,
        )

    def columns(index):
        return pl.ds(pl.multiple_of(index * TILE, TILE), TILE)

    barrier = pltpu.get_barrier_semaphore()
    for device in (across, sibling, beside):
        pl.semaphore_signal(barrier, inc=1, device_id=device, device_id_type=MESH)

    @pl.when(z < 3)
    def _():
        pl.semaphore_signal(barrier, inc=1, device_id=above, device_id_type=MESH)

    @pl.when(z > 0)
    def _():
        pl.semaphore_signal(barrier, inc=1, device_id=below, device_id_type=MESH)

    own = pltpu.make_async_copy(
        tokens.at[:, pl.ds(pl.multiple_of(x * half, 128), half)], tok.at[x, z, y], own_sem
    )
    own.start()

    def local_weight(j, a):
        src = (gate_weight, probe)[a]
        return pltpu.make_async_copy(
            src.at[:, columns(j)], weights.at[j, a, c], wl_sem.at[j, a]
        )

    @pl.loop(0, tiles)
    def _(j):
        for a in range(2):
            local_weight(j, a).start()

    cot_copy = pltpu.make_async_copy(cotangent, cot, cu_sem.at[0])
    up_copy = pltpu.make_async_copy(up_branch, up, cu_sem.at[1])
    cot_copy.start()
    up_copy.start()

    peers = 3 + jnp.minimum(z, 1) + jnp.minimum(3 - z, 1)
    pl.semaphore_wait(barrier, peers)

    def token_copy(xs, zs, sems, device):
        slot = tok.at[xs, zs, y]
        return remote(slot, slot, sems.at[xs, zs], tr_sem.at[xs, zs, y], device)

    def forward_up(xs, zs):
        @pl.when(z < 3)
        def _():
            token_copy(xs, zs, tu_sem, above).start()

    def forward_down(xs, zs):
        @pl.when(z > 0)
        def _():
            token_copy(xs, zs, td_sem, below).start()

    def token_wait(xs, zs, ys):
        slot = tok.at[xs, zs, ys]
        remote(slot, slot, ty_sem.at[xs, zs], tr_sem.at[xs, zs, ys], beside).wait_recv()

    to_across = remote(
        tokens.at[:, pl.ds(pl.multiple_of((1 - x) * half, 128), half)],
        tok.at[x, z, y], tx_sem, tr_sem.at[x, z, y], across,
    )
    to_across.start()

    def sibling_weight(j, a):
        src = (gate_weight, probe)[a]
        return remote(
            src.at[:, columns(j)], weights.at[j, a, c], ws_sem.at[j, a], wr_sem.at[j, a], sibling
        )

    def arrived_weight(j, a):
        slot = weights.at[j, a, 1 - c]
        return remote(slot, slot, ws_sem.at[j, a], wr_sem.at[j, a], sibling)

    @pl.loop(0, tiles)
    def _(j):
        for a in range(2):
            sibling_weight(j, a).start()

    own.wait()
    forward_up(x, z)
    forward_down(x, z)
    token_copy(x, z, ty_sem, beside).start()

    token_wait(1 - x, z, y)
    forward_up(1 - x, z)
    forward_down(1 - x, z)
    token_copy(1 - x, z, ty_sem, beside).start()

    def forward(d):
        @pl.when(z - d >= 0)
        def _():
            for xs in (x, 1 - x):
                token_wait(xs, z - d, y)
                forward_up(xs, z - d)
                token_copy(xs, z - d, ty_sem, beside).start()

        @pl.when(z + d <= 3)
        def _():
            for xs in (x, 1 - x):
                token_wait(xs, z + d, y)
                forward_down(xs, z + d)
                token_copy(xs, z + d, ty_sem, beside).start()

    def place(k):
        order = ((0, 1, 2, 3), (1, 0, 2, 3), (2, 1, 3, 0), (3, 2, 1, 0))
        return pick(z, [pick(k, line) for line in order])

    def partial_copy(zk, j):
        return remote(
            psend.at[zk, j], precv.at[zk, j], ps_sem.at[zk, j], pr_sem.at[zk, j], across
        )

    def sibling_tokens(xs, zk):
        return remote(
            tok.at[xs, zk, :, :, pl.ds(pl.multiple_of((1 - c) * rows, 128), rows)],
            toks2.at[xs, zk], ss_sem.at[xs, zk], sr_sem.at[xs, zk], sibling,
        )

    def product(lhs, j, a):
        return jnp.dot(
            lhs[:, :rows], weights[j, a, 0], preferred_element_type=jnp.float32
        ) + jnp.dot(lhs[:, rows:], weights[j, a, 1], preferred_element_type=jnp.float32)

    lines = part // 2

    def first_copy(ys, j):
        band = pl.ds(pl.multiple_of(ys * lines, lines), lines)
        return remote(
            psend.at[z, j, :, band], precv.at[z, j, :, band],
            fs_sem.at[ys, j], fr_sem.at[ys, j], across,
        )

    def first_half(ys, j):
        lhs = jnp.concatenate([tok[1 - x, z, ys], tok[x, z, ys]], axis=0)
        band = pl.ds(pl.multiple_of(ys * lines, lines), lines)
        for a in range(2):
            value = product(lhs, j, a)
            psend[z, j, a, band, :] = value[:lines].astype(jnp.bfloat16)
            pown[z, j, a, band, :] = value[lines:]
        first_copy(ys, j).start()

    @pl.loop(0, tiles + 2)
    def _(j):
        @pl.when(j < tiles)
        def _():
            for a in range(2):
                local_weight(j, a).wait()
                arrived_weight(j, a).wait_recv()
            first_half(y, j)

        @pl.when(j == 1)
        def _():
            forward(1)
            for xs in (x, 1 - x):
                token_wait(xs, z, 1 - y)

        @pl.when(j >= 2)
        def _():
            first_half(1 - y, j - 2)

    for xs in range(2):
        sibling_tokens(xs, z).start()

    @pl.loop(1, 4)
    def _(k):
        zk = place(k)

        for xs in (x, 1 - x):
            token_wait(xs, zk, 1 - y)

        @pl.loop(0, tiles)
        def _(j):
            @pl.when(jnp.logical_and(k < 3, j == 1))
            def _():
                forward(k + 1)

            lhs = jnp.concatenate(
                [tok[1 - x, zk].reshape(part, half), tok[x, zk].reshape(part, half)], axis=0
            )
            for a in range(2):
                value = product(lhs, j, a)
                psend[zk, j, a] = value[:part].astype(jnp.bfloat16)
                pown[zk, j, a] = value[part:]
            partial_copy(zk, j).start()

        for xs in range(2):
            sibling_tokens(xs, zk).start()

    cot_copy.wait()
    up_copy.wait()

    def weighted_copy(xs, zk, j, send, recv, device):
        slot = wall.at[xs, c, zk, j]
        return remote(slot, slot, send.at[zk, j], recv.at[zk, j], device)

    @pl.loop(0, 4)
    def _(k):
        zk = place(k)

        @pl.loop(0, tiles)
        def _(j):
            @pl.when(k == 0)
            def _():
                for ys in range(2):
                    first_copy(ys, j).wait_recv()

            @pl.when(k > 0)
            def _():
                partial_copy(zk, j).wait_recv()

            gate = pown[zk, j, 0] + precv[zk, j, 0].astype(jnp.float32)
            tangent = pown[zk, j, 1] + precv[zk, j, 1].astype(jnp.float32)
            sig = jax.nn.sigmoid(gate)
            second = sig * (1.0 - sig) * (2.0 + gate * (1.0 - 2.0 * sig))
            lines = pl.ds(pl.multiple_of(zk * part, part), part)
            wall[x, c, zk, j] = (
                cot[lines, columns(j)].astype(jnp.float32)
                * up[lines, columns(j)].astype(jnp.float32)
                * second
                * tangent
                * (1.0 / total_tokens)
            ).astype(jnp.bfloat16)
            weighted_copy(x, zk, j, vx_sem, rx_sem, across).start()
            weighted_copy(x, zk, j, vs_sem, rs_sem, sibling).start()

        mine = pl.ds(pl.multiple_of(c * rows, 128), rows)
        for xs in range(2):
            remote(
                toks2.at[xs, zk], toks2.at[xs, zk], ss_sem.at[xs, zk], sr_sem.at[xs, zk], sibling
            ).wait_recv()
        lines = [tok[xs, zk, :, :, mine].reshape(part, rows) for xs in range(2)]
        lines += [toks2[xs, zk].reshape(part, rows) for xs in range(2)]
        whole = jnp.concatenate(lines, axis=0).astype(jnp.float32)
        tok_t[k] = whole.T.astype(jnp.bfloat16)

    def arrived(xs, zk, j, recv):
        slot = wall.at[xs, 1 - c, zk, j]
        return remote(slot, slot, vs_sem.at[zk, j], recv.at[zk, j], sibling)

    def pass_on(k, j):
        zk = place(k)
        slot = wall.at[1 - x, c, zk, j]
        remote(slot, slot, vx_sem.at[zk, j], rx_sem.at[zk, j], across).wait_recv()
        weighted_copy(1 - x, zk, j, vf_sem, rf_sem, sibling).start()

    def backward(k, j):
        zk = place(k)
        arrived(x, zk, j, rs_sem).wait_recv()
        arrived(1 - x, zk, j, rf_sem).wait_recv()
        rhs = jnp.concatenate(
            [wall[0, c, zk, j], wall[1, c, zk, j], wall[0, 1 - c, zk, j], wall[1, 1 - c, zk, j]],
            axis=0,
        )
        value = jnp.dot(tok_t[k], rhs, preferred_element_type=jnp.float32)

        @pl.when(k == 0)
        def _():
            hvp[:, columns(j)] = value

        @pl.when(k > 0)
        def _():
            hvp[:, columns(j)] += value

        @pl.when(k == 0)
        def _():
            for ys in range(2):
                first_copy(ys, j).wait_send()

        @pl.when(k > 0)
        def _():
            partial_copy(zk, j).wait_send()

        weighted_copy(x, zk, j, vx_sem, rx_sem, across).wait_send()
        weighted_copy(x, zk, j, vs_sem, rs_sem, sibling).wait_send()
        weighted_copy(1 - x, zk, j, vf_sem, rf_sem, sibling).wait_send()

    to_across.wait_send()

    @pl.loop(0, tiles)
    def _(j):
        for a in range(2):
            sibling_weight(j, a).wait_send()

    @pl.loop(0, 4)
    def _(zk):
        for xs in range(2):
            token_copy(xs, zk, ty_sem, beside).wait_send()
            sibling_tokens(xs, zk).wait_send()

            @pl.when(jnp.logical_and(z < 3, zk <= z))
            def _():
                token_copy(xs, zk, tu_sem, above).wait_send()

            @pl.when(jnp.logical_and(z > 0, zk >= z))
            def _():
                token_copy(xs, zk, td_sem, below).wait_send()

    lag = 3

    @pl.loop(0, 4 * tiles + lag)
    def _(u):
        @pl.when(u < 4 * tiles)
        def _():
            pass_on(u // tiles, u % tiles)

        @pl.when(u >= lag)
        def _():
            backward((u - lag) // tiles, (u - lag) % tiles)


def small_body(tokens, cotangent, up_branch, gate_weight, probe, hess_ema):
    rows, width = gate_weight.shape
    lines = tokens.shape[0]
    part, tiles = 2 * lines, width // TILE
    bf16, f32, dma = jnp.bfloat16, jnp.float32, pltpu.SemaphoreType.DMA
    anywhere = pl.BlockSpec(memory_space=pltpu.HBM)
    grid = (4, tiles)
    hvp = pl.pallas_call(
        kernel,
        out_shape=pltpu.VMEM((rows, width), f32),
        in_specs=[anywhere] * 5,
        out_specs=pl.BlockSpec(memory_space=pltpu.VMEM),
        scratch_shapes=[
            pltpu.VMEM((tiles, 2, 2, rows, TILE), bf16),
            pltpu.VMEM((2, 4, 2, lines, 2 * rows), bf16),
            pltpu.VMEM((2, 4, 2, lines, rows), bf16),
            pltpu.VMEM((4, rows, 4 * part), bf16),
            pltpu.VMEM((4, tiles, 2, part, TILE), bf16),
            pltpu.VMEM((4, tiles, 2, part, TILE), bf16),
            pltpu.VMEM((4, tiles, 2, part, TILE), f32),
            pltpu.VMEM((2, 2, 4, tiles, part, TILE), bf16),
            pltpu.VMEM(cotangent.shape, bf16),
            pltpu.VMEM(up_branch.shape, bf16),
            dma, dma((2,)), dma((tiles, 2)), dma((tiles, 2)), dma((tiles, 2)),
            dma((2, 4, 2)), dma, dma((2, 4)), dma((2, 4)), dma((2, 4)),
            dma((2, 4)), dma((2, 4)), dma(grid), dma(grid),
            dma(grid), dma(grid), dma(grid), dma(grid), dma(grid), dma(grid),
            dma((2, tiles)), dma((2, tiles)),
        ],
        compiler_params=pltpu.CompilerParams(
            collective_id=0, has_side_effects=True, vmem_limit_bytes=44 * 1024 * 1024
        ),
        cost_estimate=pl.CostEstimate(
            flops=7_000_000_000, bytes_accessed=12_000_000, transcendentals=500_000
        ),
    )(*(
        pltpu.with_memory_space_constraint(operand, pltpu.HBM)
        for operand in (tokens, cotangent, up_branch, gate_weight, probe)
    ))
    hess_diag = probe.astype(f32) * hvp
    ema_next = 0.99 * hess_ema + 0.01 * hess_diag
    return (hess_diag, ema_next)


def body(tokens, cotangent, up_branch, gate_weight, probe, hess_ema):
    groups = lax.axis_size("fsdp")
    rows = gate_weight.shape[0]
    pieces = tokens.reshape(tokens.shape[0], groups, rows).transpose(1, 0, 2)
    pieces = lax.all_to_all(pieces, "fsdp", 0, 0, tiled=True)
    whole = lax.all_gather(pieces, "tp", axis=1, tiled=True).reshape(-1, rows)
    total_tokens = whole.shape[0]

    def summed(weight):
        part = jnp.dot(whole, weight, preferred_element_type=jnp.float32)
        return lax.psum_scatter(
            part.astype(jnp.bfloat16), "fsdp", scatter_dimension=0, tiled=True
        ).astype(jnp.float32)

    gate = summed(gate_weight)
    tangent = summed(probe)
    sig = jax.nn.sigmoid(gate)
    second = sig * (1.0 - sig) * (2.0 + gate * (1.0 - 2.0 * sig))
    weighted = (
        cotangent.astype(jnp.float32)
        * up_branch.astype(jnp.float32)
        * second
        * tangent
        / total_tokens
    ).astype(jnp.bfloat16)
    every = lax.all_gather(weighted, "fsdp", axis=0, tiled=True)
    hvp = lax.dot_general(
        whole, every, (((0,), (0,)), ((), ())), preferred_element_type=jnp.float32
    )
    hess_diag = probe.astype(jnp.float32) * hvp
    ema_next = 0.99 * hess_ema + 0.01 * hess_diag
    return (hess_diag, ema_next)


def solution(mesh):
    placed = (
        P(("fsdp", "tp"), None),
        P("fsdp", "tp"),
        P("fsdp", "tp"),
        P("fsdp", "tp"),
        P("fsdp", "tp"),
        P("fsdp", "tp"),
    )
    small = mesh.shape["fsdp"] == 4 and mesh.shape["tp"] == 8
    return jax.shard_map(
        small_body if small else body,
        mesh=mesh,
        in_specs=placed,
        out_specs=(P("fsdp", "tp"), P("fsdp", "tp")),
        check_vma=False,
    )
```
